128 devices in a mesh: leaf: 8 (over x, core), rows: 16 (over z, y).
Axes of the slice: x: 4, y: 4, z: 4, core: 2. Of those that a mesh axis runs over, the one named last changes fastest.
Arguments:
- right_side: float32 [8, 2, 64, 2048], P('leaf', None, None, 'rows'), as said below
- diag_inverse: float32 [8, 2, 2048, 128], P('leaf', None, 'rows'), as said below
- sep_lower: float32 [8, 2, 2048, 2048], P('leaf', None, 'rows'), as said below
- front_lower: float32 [8, 2, 1024, 2048], P('leaf', None, None, 'rows'), as said below
- front_index: int32 [8, 2, 1024], P('leaf'), may hold values from 0 to 6143, as said below
Outputs:
- solution: float32 [8, 2, 64, 2048], P('leaf', None, None, 'rows')
- top_update: float32 [8, 2, 64, 2048], P('leaf', None, None, 'rows')
The draws below stay inside these ranges and needn't reach their ends.
Inputs may be any that keep to these rules, and one draw needn't show every extreme that they name: `front_index`: for each leaf index and slot s the 1024 entries are distinct, lie below (3 - s) * 2048, and are the same on all 2**s leaf indices of the slot's subtree. `right_side`: entries of slot s are the same on all 2**s leaf indices of the slot's subtree. `diag_inverse`: entries of slot s are the same on all 2**s leaf indices of the slot's subtree. `sep_lower`: entries of slot s are the same on all 2**s leaf indices of the slot's subtree. `front_lower`: entries of slot s are the same on all 2**s leaf indices of the slot's subtree.
All inputs are finite; a program needn't handle non-finite values.
Results may differ from the reference program's by a relative error of at most 0.00011.
Values sent between devices are 32-bit elements; how exact they have to be, the bound alone decides.
No kernel may reach another device: no remote copies, remote signals or barrier semaphores. Data moves between devices by JAX's collectives and lax.ppermute only.
A program may use at most 128 MiB of HBM per device.

```python
from functools import partial
import jax
import jax.numpy as jnp
from jax import lax

NVEC = 64
BLK = 128
FR = 1024
LEAVES = 8
DEPTH = 3
LEVELS = 2
SEP = 2048
N_ROWS = 16


def node_blocks(key, tail, maker):
    stacked = []
    for level in range(LEVELS):
        count = LEAVES // 2 ** level
        values = maker(jax.random.fold_in(key, level), (count,) + tail)
        stacked.append(jnp.repeat(values, 2 ** level, axis=0))
    return jnp.stack(stacked, axis=1)


def right_maker(subkey, shape):
    return jnp.clip(jax.random.normal(subkey, shape, jnp.float32), -5.0, 5.0)


def draw_right_side(key, part):
    return node_blocks(key, (NVEC, SEP), right_maker)


def inverse_maker(subkey, shape):
    identity = jnp.tile(jnp.eye(BLK, dtype=jnp.float32), (SEP // BLK, 1))
    return identity + 0.4 / BLK ** 0.5 * jax.random.normal(subkey, shape, jnp.float32)


def draw_diag_inverse(key, part):
    return node_blocks(key, (SEP, BLK), inverse_maker)


def lower_maker(subkey, shape):
    return jax.random.normal(subkey, shape, jnp.float32) / SEP ** 0.5


def draw_sep_lower(key, part):
    return node_blocks(key, (SEP, SEP), lower_maker)


def front_maker(subkey, shape):
    return 0.5 * jax.random.normal(subkey, shape, jnp.float32) / SEP ** 0.5


def draw_front_lower(key, part):
    return node_blocks(key, (FR, SEP), front_maker)


def draw_front_index(key, part):
    total_width = DEPTH * SEP
    stacked = []
    for level in range(LEVELS):
        count = LEAVES // 2 ** level
        reach = (DEPTH - level) * SEP
        scores = jax.random.randint(jax.random.fold_in(key, level), (count, total_width), 0, 262144, dtype=jnp.int32)
        places = jnp.arange(total_width, dtype=jnp.int32)
        keyed = jnp.where(places[None, :] < reach, scores * total_width + places[None, :], -1)
        chosen = lax.top_k(keyed, FR)[1].astype(jnp.int32)
        stacked.append(jnp.repeat(chosen, 2 ** level, axis=0))
    return jnp.stack(stacked, axis=1)


def setup_inputs(seed: int = 0) -> dict:
    key_list = jax.random.split(jax.random.key(seed), 6)
    right_side = draw_right_side(jax.random.fold_in(key_list[5], 71), 0)
    diag_inverse = draw_diag_inverse(jax.random.fold_in(key_list[5], 71), 0)
    sep_lower = draw_sep_lower(jax.random.fold_in(key_list[5], 71), 0)
    front_lower = draw_front_lower(jax.random.fold_in(key_list[5], 71), 0)
    front_index = draw_front_index(jax.random.fold_in(key_list[5], 71), 0)
    return dict(right_side=right_side, diag_inverse=diag_inverse, sep_lower=sep_lower, front_lower=front_lower, front_index=front_index)


exact_precision = lax.Precision.HIGHEST


def product(left, right):
    return lax.dot_general(left, right, (((left.ndim - 1,), (right.ndim - 1,)), ((), ())), precision=exact_precision, preferred_element_type=jnp.float32)


def solve_rows(target, inverse, prefixes, width):
    solved = []
    for block, prefix in enumerate(prefixes):
        first = block * width
        total = target[:, first:first + width]
        if block > 0:
            total = total - product(jnp.concatenate(solved, axis=1), prefix)
        solved.append(product(total, inverse[first:first + width]))
    return jnp.concatenate(solved, axis=1)


def solve_separator(target, inverse, lower, blocks, width):
    prefixes = [lower[block * width:(block + 1) * width, :block * width] for block in range(blocks)]
    return solve_rows(target, inverse, prefixes, width)


def add_columns(held, columns, added):
    return held.at[:, columns].add(added)


def reference(right_side, diag_inverse, sep_lower, front_lower, front_index):
    pending = jnp.zeros((LEAVES, NVEC, DEPTH * SEP), jnp.float32)
    solutions = []
    solver = jax.vmap(partial(solve_separator, blocks=N_ROWS, width=BLK))
    for level in range(LEVELS):
        height = DEPTH - level
        if level > 0:
            group = 2 ** (level - 1)
            paired = pending.reshape(LEAVES // (2 * group), 2, group, NVEC, pending.shape[2])
            paired = jnp.broadcast_to(jnp.sum(paired, axis=1, keepdims=True), paired.shape)
            pending = paired.reshape(LEAVES, NVEC, paired.shape[4])
            target = right_side[:, level] - pending[:, :, height * SEP:(height + 1) * SEP]
        else:
            target = right_side[:, 0]
        pending = pending[:, :, :height * SEP]
        solved = solver(target, diag_inverse[:, level], sep_lower[:, level])
        solutions.append(solved)
        frontal = jax.vmap(product)(solved, front_lower[:, level])
        pending = jax.vmap(add_columns)(pending, front_index[:, level], frontal)
    top = pending.reshape(LEAVES, NVEC, 2, SEP).transpose(0, 2, 1, 3)
    return jnp.stack(solutions, axis=1), top
```

```python
from functools import partial

import jax
import jax.numpy as jnp
from jax import lax
from jax.experimental import pallas as pl
from jax.experimental.pallas import tpu as pltpu
from jax.sharding import PartitionSpec as P

AXES = ("leaf", "rows")
VM = pl.BlockSpec(memory_space=pltpu.VMEM)
SM = pl.BlockSpec(memory_space=pltpu.SMEM)
B = 128
NT = (((1,), (1,)), ((), ()))
NN = (((1,), (0,)), ((), ()))


def place(x, c, z, y):
    return (2 * x + c) * 16 + 4 * z + y % 4


def pairs(rule):
    found = []
    for x in range(4):
        for c in range(2):
            for z in range(4):
                for y in range(4):
                    there = rule(c, z, y)
                    if there is not None:
                        found.append((place(x, c, z, y), place(x, *there)))
    return found


def send(value, rule):
    return lax.ppermute(value, AXES, pairs(rule))


def to_line(c, z, y):
    return (1 - c, z ^ 1, y) if c != z % 2 else None


def to_line_rect(c, z, y):
    return (1, z - 1, y) if z % 2 == 1 and c == 0 else None


def to_core(c, z, y):
    return (1 - c, z, y)


def from_second_core(c, z, y):
    return (0, z, y) if c == 1 else None


def along(k, second_only=False):
    def rule(c, z, y):
        return (c, z, y + k) if c == 1 or not second_only else None

    return rule


def coupling_to_top(c, z, y):
    return (z - 2, c, y) if z >= 2 else None


def top_to_bottom(k):
    def rule(c, z, y):
        return (c, z + 2, y + k) if z < 2 else None

    return rule


def ring(block, second_only):
    rows = block.shape[0] // 2
    up = send(block, along(1, second_only))
    down = send(block, along(3, second_only))
    far_low = send(up[:rows], along(1, second_only))
    far_high = send(down[rows:], along(3, second_only))
    return [block, up, down, far_low, far_high]


def halves(value):
    high = value.astype(jnp.bfloat16)
    low = (value - high.astype(jnp.float32)).astype(jnp.bfloat16)
    return high, low


def dot(left, right, dims=NN):
    return lax.dot_general(left, right, dims, preferred_element_type=jnp.float32)


def times(left, right, dims=NN):
    lh, ll = left if isinstance(left, tuple) else halves(left)
    rh, rl = right if isinstance(right, tuple) else halves(right)
    return dot(lh, rh, dims) + (dot(lh, rl, dims) + dot(ll, rh, dims))


def lanes(block):
    return pl.ds(pl.multiple_of(block * B, B), B)


def factor_kernel(first, where, *refs):
    own, other = refs[0:5], refs[5:10]
    rect_own, rect_other = refs[10:15], refs[15:20]
    coupling = refs[20]
    fronts = refs[21:25]
    outs = refs[25:28] if first else refs[25:27]
    tri, rect, w = refs[-3:]
    c = where[0]
    y = where[1]

    def fill(target, base, parts):
        rows = parts[0].shape[0]
        half = rows // 2
        target[base + y] = parts[0][...]
        target[base + lax.rem(y + 3, 4)] = parts[1][...]
        target[base + lax.rem(y + 1, 4)] = parts[2][...]
        far = base + lax.rem(y + 2, 4)
        target[far, pl.ds(0, half)] = parts[3][...]
        target[far, pl.ds(half, half)] = parts[4][...]

    fill(tri, 4 * c, own)
    fill(tri, 4 * (1 - c), other)

    @pl.when(c == 1)
    def _():
        fill(rect, 0, rect_own)

    @pl.when(c == 0)
    def _():
        fill(rect, 0, rect_other)

    w[0:B, :] = coupling[...]
    for k in range(4):
        col = lax.rem(y + 4 - k, 4)
        w[B : 2 * B, lanes(col)] = fronts[k][:, 0:B]
        w[B : 2 * B, lanes(4 + col)] = fronts[k][:, B : 2 * B]
    w[2 * B : 3 * B, :] = jnp.zeros((B, 8 * B), jnp.float32)
    row = lax.broadcasted_iota(jnp.int32, (B, B), 0)
    col = lax.broadcasted_iota(jnp.int32, (B, B), 1)
    w[2 * B : 3 * B, lanes(4 * c + y)] = jnp.where(row == col, 1.0, 0.0)

    def pair_inverse(m):
        a, b = 2 * m, 2 * m + 1
        da = tri[a, 0:B, 3 * B : 4 * B]
        db = tri[b, 0:B, 3 * B : 4 * B]
        k = (a % 4) * B
        below = -times(times(db, tri[b, 0:B, k : k + B]), da)
        upper = jnp.concatenate([da, jnp.zeros((B, B), jnp.float32)], axis=1)
        lower = jnp.concatenate([below, db], axis=1)
        return halves(jnp.concatenate([upper, lower], axis=0))

    def block(m, n):
        a = 2 * m
        if m // 2 == n // 2:
            return halves(jnp.concatenate([tri[a, 0:B, 0 : 2 * B], tri[a + 1, 0:B, 0 : 2 * B]], axis=0))
        k = n * 2 * B
        return halves(jnp.concatenate([rect[a - 4, :, k : k + 2 * B], rect[a - 3, :, k : k + 2 * B]], axis=0))

    inverses = [pair_inverse(m) for m in range(4)]
    solved = {}
    for m in (3, 2, 1, 0):
        total = w[:, 2 * B * m : 2 * B * (m + 1)]
        for n in range(m + 1, 4):
            total = total - times(solved[n], block(n, m))
        value = times(total, inverses[m])
        outs[0][:, 2 * B * m : 2 * B * (m + 1)] = value
        solved[m] = halves(value)
    for i in range(8):
        for a in range(4):
            outs[1][16 * a : 16 * a + 16, B * i : B * (i + 1)] = tri[i, B : B + 16, B * a : B * (a + 1)]
    if first:
        total = None
        for m in range(4):
            part = times(outs[1][:, 2 * B * m : 2 * B * (m + 1)], solved[m], NT)
            total = part if total is None else total + part
        outs[2][...] = total


def factor(first, where, pieces):
    vectors = 64
    shapes = [
        jax.ShapeDtypeStruct((3 * B, 8 * B), jnp.float32),
        jax.ShapeDtypeStruct((vectors, 8 * B), jnp.float32),
    ]
    if first:
        shapes.append(jax.ShapeDtypeStruct((vectors, 3 * B), jnp.float32))
    return pl.pallas_call(
        partial(factor_kernel, first),
        out_shape=shapes,
        in_specs=[SM] + [VM] * len(pieces),
        out_specs=[VM] * len(shapes),
        scratch_shapes=[
            pltpu.VMEM((8, B + 16, 4 * B), jnp.float32),
            pltpu.VMEM((4, B, 4 * B), jnp.float32),
            pltpu.VMEM((3 * B, 8 * B), jnp.float32),
        ],
        compiler_params=pltpu.CompilerParams(vmem_limit_bytes=48 * 2**20),
        name="factor",
    )(where, *pieces)


def apply_matrix(target, matrix):
    total = None
    for m in range(4):
        cols = slice(2 * B * m, 2 * B * (m + 1))
        part = times(target[:, cols], matrix[:, cols], NT)
        total = part if total is None else total + part
    return total


def bottom_kernel(where, target, matrix, top, u1, u2, u3, out, t):
    y = where[1]
    for k, u in enumerate((top, u1, u2, u3)):
        col = lax.rem(y + 4 - k, 4)
        for c in range(2):
            at = lanes(4 * c + col)
            t[:, at] = target[:, at] - u[:, B * c : B * (c + 1)]
    value = apply_matrix(t, matrix)
    out[:, 0:B] = value[:, B : 2 * B] + top[:, 2 * B : 3 * B]
    out[:, B : 2 * B] = value[:, 2 * B : 3 * B]


def bottom(where, target, matrix, received):
    return pl.pallas_call(
        bottom_kernel,
        out_shape=jax.ShapeDtypeStruct((64, 2 * B), jnp.float32),
        in_specs=[SM] + [VM] * 6,
        out_specs=VM,
        scratch_shapes=[pltpu.VMEM((64, 8 * B), jnp.float32)],
        compiler_params=pltpu.CompilerParams(vmem_limit_bytes=32 * 2**20),
        name="bottom",
    )(where, target, matrix, *received)


def thirds(value):
    high, rest = halves(value)
    middle = value - high.astype(jnp.float32)
    low = (middle - rest.astype(jnp.float32)).astype(jnp.bfloat16)
    return jnp.concatenate([high, rest, low], axis=0)


def spread(values, index, base, width):
    lhs = jnp.concatenate([thirds(v) for v in values], axis=1)
    col = lax.broadcasted_iota(jnp.int32, (index.shape[0], width), 1) + base
    chosen = jnp.where(index == col, 1.0, 0.0).astype(jnp.bfloat16)
    laid = dot(lhs, chosen)
    n = values[0].shape[0]
    return laid[0:n] + (laid[n : 2 * n] + laid[2 * n : 3 * n])


def middle_kernel(where, target, matrix, mine, theirs, index, t_out, out):
    c = where[0]
    base = 2 * 2048 + where[2] * 1024
    total = target[...]
    for q in range(2):
        for e in range(2):
            source = mine if e == 0 else theirs
            core = c if e == 0 else 1 - c
            for half in range(2):
                j = 4 * q + 2 * half
                rows = pl.ds(pl.multiple_of(1024 * q + 512 * core + 256 * half, 256), 256)
                total = total - spread([source[j], source[j + 1]], index[rows, :], base, 8 * B)
    t_out[...] = total
    out[...] = apply_matrix(total, matrix)


def middle(where, target, matrix, mine, theirs, index):
    return pl.pallas_call(
        middle_kernel,
        out_shape=[
            jax.ShapeDtypeStruct((64, 8 * B), jnp.float32),
            jax.ShapeDtypeStruct((64, 3 * B), jnp.float32),
        ],
        in_specs=[SM] + [VM] * 5,
        out_specs=[VM] * 2,
        compiler_params=pltpu.CompilerParams(vmem_limit_bytes=48 * 2**20),
        name="middle",
    )(where, target, matrix, mine, theirs, index)


def last_kernel(where, mine, theirs, index, mine1, theirs1, index1, out):
    c = where[0]
    here = where[3]
    for t in range(2):
        base = t * 2048 + here * B
        total = None
        for e in range(2):
            core = c if e == 0 else 1 - c
            for half in range(2):
                source = mine if e == 0 else theirs
                for q in range(2):
                    j = 4 * q + 2 * half
                    rows = pl.ds(pl.multiple_of(1024 * q + 512 * core + 256 * half, 256), 256)
                    part = spread([source[j], source[j + 1]], index[rows, :], base, B)
                    total = part if total is None else total + part
                source = mine1 if e == 0 else theirs1
                j = 2 * half
                rows = pl.ds(pl.multiple_of(512 * core + 256 * half, 256), 256)
                total = total + spread([source[j], source[j + 1]], index1[rows, :], base, B)
        out[t] = total


def last(where, mine, theirs, index, mine1, theirs1, index1):
    return pl.pallas_call(
        last_kernel,
        out_shape=jax.ShapeDtypeStruct((2, 64, B), jnp.float32),
        in_specs=[SM] + [VM] * 6,
        out_specs=VM,
        compiler_params=pltpu.CompilerParams(vmem_limit_bytes=48 * 2**20),
        name="last",
    )(where, mine, theirs, index, mine1, theirs1, index1)


def on_device(right_side, diag_inverse, sep_lower, front_lower, front_index):
    leaf = lax.axis_index("leaf")
    here = lax.axis_index("rows")
    c = lax.rem(leaf, 2)
    z = here // 4
    y = lax.rem(here, 4)
    h = z // 2
    stays = c == lax.rem(z, 2)
    where = jnp.stack([c, y, h, here]).astype(jnp.int32)

    index_other = send(front_index[0, 0], to_core)
    index0 = jnp.where(
        c == 0,
        jnp.concatenate([front_index[0, 0], index_other]),
        jnp.concatenate([index_other, front_index[0, 0]]),
    )[:, None]
    index1 = front_index[0, 1][:, None]

    def gathered(s, first):
        lower = sep_lower[0, s]
        near = lax.dynamic_slice_in_dim(lower, h * 1024 + lax.rem(z, 2) * 512, 3 * B, 1)
        right = right_side[0, s]
        right = jnp.concatenate([right[16 * a : 16 * a + 16] for a in range(4)], axis=1)
        tri = jnp.concatenate([jnp.concatenate([near, diag_inverse[0, s]], axis=1), right], axis=0)
        rect = lax.dynamic_slice_in_dim(lower, h * 1024, 4 * B, 1)
        tri = jnp.where(stays, tri, send(tri, to_line))
        rect = jnp.where(stays, rect, send(rect, to_line_rect))
        tri_parts = ring(tri, False)
        rect_parts = ring(rect, True)
        tri_others = [send(p, to_core) for p in tri_parts]
        rect_others = [send(p, from_second_core) for p in rect_parts]
        coupling = send(lower[:, :1024], coupling_to_top)
        front = front_lower[0, s]
        front = jnp.where(stays, front, send(front, to_line))
        kept = lax.dynamic_slice_in_dim(front, 512 * c, 512, 0)
        given = lax.dynamic_slice_in_dim(front, 512 * (1 - c), 512, 0)
        taken = send(given, to_core)
        both = jnp.where(
            c == 0,
            jnp.concatenate([kept, taken], axis=1),
            jnp.concatenate([taken, kept], axis=1),
        )
        fronts = []
        for k in range(4):
            slab = lax.dynamic_slice_in_dim(both, lax.rem(y + k, 4) * B, B, 0)
            fronts.append(slab if k == 0 else send(slab, along(k)))
        pieces = [*tri_parts, *tri_others, *rect_parts, *rect_others, coupling, *fronts]
        return factor(first, where, pieces)

    def to_bottom(out):
        other = send(out[:, :B], to_core)
        u = jnp.where(
            c == 0,
            jnp.concatenate([out[:, :B], other], axis=1),
            jnp.concatenate([other, out[:, :B]], axis=1),
        )
        top = send(jnp.concatenate([u, out[:, B : 2 * B]], axis=1), top_to_bottom(0))
        return [top] + [send(u, top_to_bottom(k)) for k in range(1, 4)]

    def to_all(part, count):
        copies = jnp.broadcast_to(part, (16, *part.shape))
        mine = lax.all_to_all(copies, "rows", 0, 0, tiled=True)[8 : 8 + count]
        return mine, send(mine, to_core)

    matrix0, target0, out0 = gathered(0, True)
    matrix1, target1 = gathered(1, False)
    done0 = bottom(where, target0, matrix0, to_bottom(out0))
    mine0, theirs0 = to_all(done0[:, :B], 8)
    target1, out1 = middle(where, target1, matrix1, mine0, theirs0, index0)
    done1 = bottom(where, target1, matrix1, to_bottom(out1))
    mine1, theirs1 = to_all(done1[:, :B], 4)
    top = last(where, mine0, theirs0, index0, mine1, theirs1, index1)
    solved = jnp.stack([done0[:, B:], done1[:, B:]])
    solved = jnp.where(stays, solved, send(solved, to_line))
    return solved[None], top[None]


def solution(mesh):
    in_specs = (
        P("leaf", None, None, "rows"),
        P("leaf", None, "rows", None),
        P("leaf", None, "rows", None),
        P("leaf", None, None, "rows"),
        P("leaf", None, None),
    )
    out_specs = (P("leaf", None, None, "rows"), P("leaf", None, None, "rows"))
    return jax.shard_map(
        on_device, mesh=mesh, in_specs=in_specs, out_specs=out_specs, check_vma=False
    )
```

```python
from functools import partial

import jax
import jax.numpy as jnp
from jax import lax
from jax.experimental import pallas as pl
from jax.experimental.pallas import tpu as pltpu
from jax.sharding import PartitionSpec as P

AXES = ("leaf", "rows")
VM = pl.BlockSpec(memory_space=pltpu.VMEM)
HB = pl.BlockSpec(memory_space=pltpu.HBM)
AN = pl.BlockSpec(memory_space=pl.ANY)
SM = pl.BlockSpec(memory_space=pltpu.SMEM)
B = 128
NT = (((1,), (1,)), ((), ()))
NN = (((1,), (0,)), ((), ()))


def place(x, c, z, y):
    return (2 * x + c) * 16 + 4 * z + y % 4


def pairs(rule):
    found = []
    for x in range(4):
        for c in range(2):
            for z in range(4):
                for y in range(4):
                    there = rule(c, z, y)
                    if there is not None:
                        found.append((place(x, c, z, y), place(x, *there)))
    return found


def send(value, rule):
    return lax.ppermute(value, AXES, pairs(rule))


def to_line(c, z, y):
    h = z // 2
    return ((z % 2) ^ h, 2 * h + (c ^ h), y)


def left_to_line(c, z, y):
    h = z // 2
    return (h, 2 * h + (c ^ h), y) if z % 2 == 1 else None


def to_core(c, z, y):
    return (1 - c, z, y)


def along(k):
    def rule(c, z, y):
        return (c, z, y + k)

    return rule


def coupling_to_top(c, z, y):
    return (z - 2, c, y) if z >= 2 else None


def top_to_bottom(k):
    def rule(c, z, y):
        return (c, 3 - z, y + k) if z < 2 else None

    return rule


def halves(value):
    high = value.astype(jnp.bfloat16)
    low = (value - high.astype(jnp.float32)).astype(jnp.bfloat16)
    return high, low


def dot(left, right, dims=NN):
    return lax.dot_general(left, right, dims, preferred_element_type=jnp.float32)


def times(left, right, dims=NN):
    lh, ll = left if isinstance(left, tuple) else halves(left)
    rh, rl = right if isinstance(right, tuple) else halves(right)
    return dot(lh, rh, dims) + (dot(lh, rl, dims) + dot(ll, rh, dims))


def lanes(block):
    return pl.ds(pl.multiple_of(block * B, B), B)


def run_copies(copies, sems):
    for copy in start_all(copies, sems):
        copy.wait()


def message_copies(where, s, right, inverse, lower, main, left):
    base = 1024 * where[2]
    cols = pl.ds(0, B)
    copies = [
        (lower.at[s, :, cut(base + 512 * where[5], 3 * B)], main.at[s, cols, pl.ds(0, 3 * B)]),
        (inverse.at[s], main.at[s, cols, pl.ds(3 * B, B)]),
        (lower.at[s, :, cut(base + 256, 2 * B)], main.at[s, cols, pl.ds(4 * B, 2 * B)]),
        (lower.at[s, :, cut(base, 2 * B)], left.at[s]),
    ]
    for k in range(4):
        copies.append((right.at[s, pl.ds(16 * k, 16)], main.at[s, pl.ds(B, 16), pl.ds(B * k, B)]))
    return copies


def pack_kernel(where, right, inverse, lower, main, left, sems):
    copies = []
    for s in range(2):
        copies += message_copies(where, s, right, inverse, lower, main, left)
    started = start_all(copies, sems)
    for s in range(2):
        main[s, B : B + 16, 4 * B : 6 * B] = jnp.zeros((16, 2 * B), jnp.float32)
    for copy in started:
        copy.wait()


def rest_kernel(where, lower, front, dep, couple, fronts, sems):
    rows = rows_of(64 * where[6], 64)
    run_copies(
        [
            (lower.at[:, :, pl.ds(0, 8 * B)], couple),
            (front.at[0], fronts.at[:, pl.ds(0, B)]),
            (front.at[1, :, rows], fronts.at[:, pl.ds(B, 64)]),
        ],
        sems,
    )


def own_kernel(where, main, left, *refs):
    own = refs[-1]
    own[:, :, 0 : 4 * B] = main[:, :, 0 : 4 * B]

    @pl.when(where[0] == 0)
    def _():
        own[:, 0:B, 4 * B :] = left[...]
        own[:, B:, 4 * B :] = jnp.zeros((2, 16, 2 * B), jnp.float32)

    @pl.when(where[0] == 1)
    def _():
        own[:, :, 4 * B :] = main[:, :, 4 * B :]


def pass_kernel(value, dep, out):
    pass


def gate(value, dep):
    return pl.pallas_call(
        pass_kernel,
        out_shape=jax.ShapeDtypeStruct(value.shape, value.dtype),
        in_specs=[AN] * 2,
        out_specs=AN,
        input_output_aliases={0: 0},
        name="gate",
    )(value, dep)


def cut(start, size):
    return pl.ds(pl.multiple_of(start, B), size)


def rows_of(start, size):
    return pl.ds(pl.multiple_of(start, 64), size)


def f32(*shape):
    return jax.ShapeDtypeStruct(shape, jnp.float32)


def pack(where, right, inverse, lower):
    return pl.pallas_call(
        pack_kernel,
        out_shape=[f32(2, B + 16, 6 * B), f32(2, B, 2 * B)],
        in_specs=[SM] + [HB] * 3,
        out_specs=[VM] * 2,
        scratch_shapes=[pltpu.SemaphoreType.DMA((16,))],
        name="pack",
    )(where, right, inverse, lower)


def rest(where, lower, front, dep):
    return pl.pallas_call(
        rest_kernel,
        out_shape=[f32(2, B, 8 * B), f32(8, B + 64, B)],
        in_specs=[SM] + [HB] * 2 + [AN],
        out_specs=[VM] * 2,
        scratch_shapes=[pltpu.SemaphoreType.DMA((3,))],
        name="rest",
    )(where, lower, front, dep)


def own_piece(where, main, left, *dep):
    return pl.pallas_call(
        own_kernel,
        out_shape=f32(2, B + 16, 6 * B),
        in_specs=[SM] + [VM] * 2 + [AN] * len(dep),
        out_specs=VM,
        name="own",
    )(where, main, left, *dep)


def solve_factor(stage, w, matrix):
    def pair_inverse(m):
        i = 2 * m
        k = i % 4
        upper = stage[i, 0:B, 3 * B : 4 * B]
        lower = stage[i + 1, 0:B, 3 * B : 4 * B]
        below = -times(times(lower, stage[i + 1, 0:B, B * k : B * (k + 1)]), upper)
        zeros = jnp.zeros((B, B), jnp.float32)
        return halves(
            jnp.concatenate(
                [jnp.concatenate([upper, zeros], axis=1), jnp.concatenate([below, lower], axis=1)],
                axis=0,
            )
        )

    def block(m, n):
        i = 2 * m
        if m // 2 == n // 2:
            cols = slice(0, 2 * B)
        else:
            i = i - 4 if n == 0 else i
            cols = slice(4 * B, 6 * B)
        return halves(jnp.concatenate([stage[i, 0:B, cols], stage[i + 1, 0:B, cols]], axis=0))

    inverses = [pair_inverse(m) for m in range(4)]
    solved = {}
    for m in (3, 2, 1, 0):
        total = w[:, 2 * B * m : 2 * B * (m + 1)]
        for n in range(m + 1, 4):
            total = total - times(solved[n], block(n, m))
        value = times(total, inverses[m])
        if matrix is not None:
            matrix[:, 2 * B * m : 2 * B * (m + 1)] = value
        solved[m] = halves(value)
    return solved


def coupling_copies(s, w, c, coupling, coupling_other):
    return [
        (coupling.at[s], w.at[cut(B * c, B), :]),
        (coupling_other.at[s], w.at[cut(B * (1 - c), B), :]),
    ]


def front_copies(w, at, front):
    return [(front.at[i], w.at[pl.ds(at, B), pl.ds(B * i, B)]) for i in range(8)]


def shared_copies(w, at, c, mine, theirs):
    copies = []
    for i in range(8):
        cols = pl.ds(B * i, B)
        copies.append((mine.at[i, pl.ds(B, 64)], w.at[rows_of(at + 64 * c, 64), cols]))
        copies.append((theirs.at[i], w.at[rows_of(at + 64 * (1 - c), 64), cols]))
    return copies


def own_rows(w, at, own_row):
    w[at : at + B, :] = jnp.zeros((B, 8 * B), jnp.float32)
    row = lax.broadcasted_iota(jnp.int32, (B, B), 0)
    col = lax.broadcasted_iota(jnp.int32, (B, B), 1)
    w[at : at + B, lanes(own_row)] = jnp.where(row == col, 1.0, 0.0)


def start_all(copies, sems):
    started = [pltpu.make_async_copy(src, dst, sems.at[n]) for n, (src, dst) in enumerate(copies)]
    for copy in started:
        copy.start()
    return started


def factor_kernel(s, where, *refs):
    c = where[6]
    a = where[0]
    y = where[1]
    if s == 0:
        matrix, right, u, stage, w, sems = refs[13:]
        copies = front_copies(w, 2 * B, refs[12])
    else:
        matrix, right, stage, w, sems = refs[15:]
        copies = shared_copies(w, 2 * B, c, *refs[12:14])
    copies += coupling_copies(s, w, c, *refs[10:12])
    own_rows(w, 3 * B, where[4])
    half = (B + 16) // 2
    for g, parts in ((a, refs[0:5]), (1 - a, refs[5:10])):
        parts = [part.at[s] for part in parts]
        copies.append((parts[0], stage.at[4 * g + y]))
        copies.append((parts[1], stage.at[4 * g + lax.rem(y + 3, 4)]))
        copies.append((parts[2], stage.at[4 * g + lax.rem(y + 1, 4)]))
        far = 4 * g + lax.rem(y + 2, 4)
        copies.append((parts[3], stage.at[far, pl.ds(0, half)]))
        copies.append((parts[4], stage.at[far, pl.ds(half, half)]))
    for copy in start_all(copies, sems):
        copy.wait()
    solved = solve_factor(stage, w, matrix)
    for i in range(8):
        for k in range(4):
            right[16 * k : 16 * k + 16, B * i : B * (i + 1)] = stage[i, B : B + 16, B * k : B * (k + 1)]
    if s == 1:
        return
    total = None
    for m in range(4):
        high, low = solved[m]
        part = (high[0 : 2 * B], low[0 : 2 * B])
        part = times(right[:, 2 * B * m : 2 * B * (m + 1)], part, NT)
        total = part if total is None else total + part
    u[...] = total


def factor(s, where, pieces):
    shapes = [f32(4 * B, 8 * B), f32(64, 8 * B)]
    if s == 0:
        shapes.append(f32(64, 2 * B))
    return pl.pallas_call(
        partial(factor_kernel, s),
        out_shape=shapes,
        in_specs=[SM] + [HB] * len(pieces),
        out_specs=[VM] * len(shapes),
        scratch_shapes=[
            pltpu.VMEM((8, B + 16, 6 * B), jnp.float32),
            pltpu.VMEM((4 * B, 8 * B), jnp.float32),
            pltpu.SemaphoreType.DMA((28,)),
        ],
        compiler_params=pltpu.CompilerParams(vmem_limit_bytes=32 * 2**20),
        name="factor",
    )(where, *pieces)


def apply_matrix(target, matrix, rows):
    total = None
    for m in range(4):
        cols = slice(2 * B * m, 2 * B * (m + 1))
        part = times(target[:, cols], matrix[rows, cols], NT)
        total = part if total is None else total + part
    return total


def bottom_kernel(where, target, matrix, u0, u1, u2, u3, *refs):
    front, solved, t = refs[-3:]
    y = where[1]
    for k, u in enumerate((u0, u1, u2, u3)):
        col = lax.rem(y + 4 - k, 4)
        for g in range(2):
            at = lanes(4 * g + col)
            t[:, at] = target[:, at] - u[:, B * g : B * (g + 1)]
    last = matrix.shape[0]
    value = apply_matrix(t, matrix, slice(last - 2 * B, last))
    for k in range(16):
        front[k] = value[:, 0:B]
    solved[...] = value[:, B : 2 * B]


def bottom(where, target, matrix, received, *dep):
    return pl.pallas_call(
        bottom_kernel,
        out_shape=[
            jax.ShapeDtypeStruct((16, 64, B), jnp.float32),
            jax.ShapeDtypeStruct((64, B), jnp.float32),
        ],
        in_specs=[SM] + [VM] * 6 + [AN] * len(dep),
        out_specs=[VM] * 2,
        scratch_shapes=[pltpu.VMEM((64, 8 * B), jnp.float32)],
        compiler_params=pltpu.CompilerParams(vmem_limit_bytes=20 * 2**20),
        name="bottom",
    )(where, target, matrix, *received, *dep)


def thirds(value):
    high, rest = halves(value)
    middle = value - high.astype(jnp.float32)
    low = (middle - rest.astype(jnp.float32)).astype(jnp.bfloat16)
    return jnp.concatenate([high, rest, low], axis=0)


def spread(values, index, base, width):
    lhs = jnp.concatenate([thirds(v) for v in values], axis=1)
    col = lax.broadcasted_iota(jnp.int32, (index.shape[0], width), 1) + base
    chosen = jnp.where(index == col, 1.0, 0.0).astype(jnp.bfloat16)
    laid = dot(lhs, chosen)
    n = values[0].shape[0]
    return laid[0:n] + (laid[n : 2 * n] + laid[2 * n : 3 * n])


def first_fronts(c, mine, theirs):
    for q in range(2):
        for e, (upper, lower) in enumerate(((mine, theirs), (theirs, mine))):
            group = c if e == 0 else 1 - c
            for y in (0, 2):
                values = [upper[4 * q + k] + lower[4 * (3 - q) + k] for k in (y, y + 1)]
                yield values, cut(1024 * q + 512 * group + B * y, 2 * B)


def middle_kernel(where, target, matrix, mine, theirs, index, t_out, u):
    base = 2 * 2048 + where[2] * 1024
    total = target[...]
    for values, rows in first_fronts(where[6], mine, theirs):
        total = total - spread(values, index[rows, :], base, 8 * B)
    t_out[...] = total
    u[...] = apply_matrix(total, matrix, slice(0, 2 * B))


def middle(where, target, matrix, mine, theirs, index):
    return pl.pallas_call(
        middle_kernel,
        out_shape=[
            jax.ShapeDtypeStruct((64, 8 * B), jnp.float32),
            jax.ShapeDtypeStruct((64, 2 * B), jnp.float32),
        ],
        in_specs=[SM] + [VM] * 5,
        out_specs=[VM] * 2,
        compiler_params=pltpu.CompilerParams(vmem_limit_bytes=24 * 2**20),
        name="middle",
    )(where, target, matrix, mine, theirs, index)


def older_kernel(where, mine, theirs, index, out):
    for t in range(2):
        total = None
        for values, rows in first_fronts(where[6], mine, theirs):
            part = spread(values, index[rows, :], t * 2048 + where[3] * B, B)
            total = part if total is None else total + part
        out[t] = total


def older(where, mine, theirs, index):
    return pl.pallas_call(
        older_kernel,
        out_shape=f32(2, 64, B),
        in_specs=[SM] + [VM] * 3,
        out_specs=VM,
        compiler_params=pltpu.CompilerParams(vmem_limit_bytes=24 * 2**20),
        name="older",
    )(where, mine, theirs, index)


def last_kernel(where, held, mine, index, out):
    for t in range(2):
        total = held[t]
        for j in range(0, 8, 2):
            values = [mine[k] + mine[8 + k] for k in (j, j + 1)]
            total = total + spread(values, index[B * j : B * (j + 2), :], t * 2048 + where[3] * B, B)
        out[t] = total


def last(where, held, mine, index):
    return pl.pallas_call(
        last_kernel,
        out_shape=f32(2, 64, B),
        in_specs=[SM] + [VM] * 3,
        out_specs=VM,
        compiler_params=pltpu.CompilerParams(vmem_limit_bytes=24 * 2**20),
        name="last",
    )(where, held, mine, index)


HALVES = [list(range(8)), list(range(8, 16))]


def on_device(right_side, diag_inverse, sep_lower, front_lower, front_index):
    leaf = lax.axis_index("leaf")
    here = lax.axis_index("rows")
    c = lax.rem(leaf, 2)
    z = here // 4
    y = lax.rem(here, 4)
    h = z // 2
    odd = lax.rem(z, 2)
    a = lax.rem(c + h, 2)
    where = jnp.stack([a, y, h, here, 4 * a + y, odd, c, 4 * odd + y]).astype(jnp.int32)

    right, inverse, lower, front = right_side[0], diag_inverse[0], sep_lower[0], front_lower[0]
    front = front.reshape(2, 8, B, B)

    index = front_index[0, 0]
    index_other = send(index, to_core)
    index0 = jnp.where(
        c == 0,
        jnp.concatenate([index, index_other]),
        jnp.concatenate([index_other, index]),
    )[:, None]
    index1 = front_index[0, 1][:, None]

    main, left = pack(where, right, inverse, lower)
    couple, fronts = rest(where, lower, front, main)
    main = send(main, to_line)
    left = send(left, left_to_line)
    own = own_piece(where, main, left, couple, fronts, index0, index1)
    size = own.shape[1] // 2
    up = send(own, along(1))
    down = send(own, along(3))
    far_low = send(up[:, :size], along(1))
    far_high = send(down[:, size:], along(3))
    pieces = [own, up, down, far_low, far_high]
    pieces += [send(p, to_core) for p in pieces]
    couple = send(gate(couple, own), coupling_to_top)
    pieces += [couple, send(couple, to_core)]
    fronts = gate(fronts, own)
    fronts = lax.all_to_all(fronts, "rows", 0, 0, axis_index_groups=HALVES, tiled=True)
    front0 = send(fronts[:, :B], to_line)
    front1 = send(fronts[:, B:], to_core)

    matrix0, target0, u0 = factor(0, where, [*pieces, front0])
    received = [send(u0, top_to_bottom(k)) for k in range(4)]
    matrix1, target1 = factor(1, where, [*pieces, fronts, front1, u0])
    done0, solved0 = bottom(where, target0, matrix0, received, target1)
    mine0 = lax.all_to_all(done0, "rows", 0, 0, tiled=True)
    theirs0 = send(mine0, to_core)

    target1, u1 = middle(where, target1, matrix1, mine0, theirs0, index0)
    received = [send(u1, top_to_bottom(k)) for k in range(4)]
    done1, solved1 = bottom(where, target1, matrix1, received)
    mine1 = lax.all_to_all(done1, "rows", 0, 0, tiled=True)
    top = last(where, older(where, mine0, theirs0, index0), mine1, index1)
    solved = send(jnp.stack([solved0, solved1]), to_line)
    return solved[None], top[None]


def solution(mesh):
    in_specs = (
        P("leaf", None, None, "rows"),
        P("leaf", None, "rows", None),
        P("leaf", None, "rows", None),
        P("leaf", None, None, "rows"),
        P("leaf", None, None),
    )
    out_specs = (P("leaf", None, None, "rows"), P("leaf", None, None, "rows"))
    return jax.shard_map(
        on_device, mesh=mesh, in_specs=in_specs, out_specs=out_specs, check_vma=False
    )
```

```python
from functools import partial

import jax
import jax.numpy as jnp
from jax import lax
from jax.experimental import pallas as pl
from jax.experimental.pallas import tpu as pltpu
from jax.sharding import PartitionSpec as P

AXES = ("leaf", "rows")
VM = pl.BlockSpec(memory_space=pltpu.VMEM)
HB = pl.BlockSpec(memory_space=pltpu.HBM)
AN = pl.BlockSpec(memory_space=pl.ANY)
SM = pl.BlockSpec(memory_space=pltpu.SMEM)
B = 128
NT = (((1,), (1,)), ((), ()))
NN = (((1,), (0,)), ((), ()))


def place(x, c, z, y):
    return (2 * x + c) * 16 + 4 * z + y % 4


def pairs(rule):
    found = []
    for x in range(4):
        for c in range(2):
            for z in range(4):
                for y in range(4):
                    there = rule(c, z, y)
                    if there is not None:
                        found.append((place(x, c, z, y), place(x, *there)))
    return found


def send(value, rule):
    return lax.ppermute(value, AXES, pairs(rule))


def to_line(c, z, y):
    h = z // 2
    return ((z % 2) ^ h, 2 * h + (c ^ h), y)


def left_to_line(c, z, y):
    h = z // 2
    return (h, 2 * h + (c ^ h), y) if z % 2 == 1 else None


def to_core(c, z, y):
    return (1 - c, z, y)


def along(k):
    def rule(c, z, y):
        return (c, z, y + k)

    return rule


def coupling_to_top(c, z, y):
    return (z - 2, c, y) if z >= 2 else None


def top_to_bottom(k):
    def rule(c, z, y):
        return (c, 3 - z, y + k) if z < 2 else None

    return rule


def halves(value):
    high = value.astype(jnp.bfloat16)
    low = (value - high.astype(jnp.float32)).astype(jnp.bfloat16)
    return high, low


def dot(left, right, dims=NN):
    return lax.dot_general(left, right, dims, preferred_element_type=jnp.float32)


def times(left, right, dims=NN):
    lh, ll = left if isinstance(left, tuple) else halves(left)
    rh, rl = right if isinstance(right, tuple) else halves(right)
    return dot(lh, rh, dims) + (dot(lh, rl, dims) + dot(ll, rh, dims))


def lanes(block):
    return pl.ds(pl.multiple_of(block * B, B), B)


def run_copies(copies, sems):
    for copy in start_all(copies, sems):
        copy.wait()


def message_copies(where, s, right, inverse, lower, main, left):
    base = 1024 * where[2]
    cols = pl.ds(0, B)
    copies = [
        (lower.at[s, :, cut(base + 512 * where[5], 3 * B)], main.at[s, cols, pl.ds(0, 3 * B)]),
        (inverse.at[s], main.at[s, cols, pl.ds(3 * B, B)]),
        (lower.at[s, :, cut(base + 256, 2 * B)], main.at[s, cols, pl.ds(4 * B, 2 * B)]),
        (lower.at[s, :, cut(base, 2 * B)], left.at[s]),
    ]
    for k in range(4):
        copies.append((right.at[s, pl.ds(16 * k, 16)], main.at[s, pl.ds(B, 16), pl.ds(B * k, B)]))
    return copies


def pack_kernel(where, right, inverse, lower, main, left, sems):
    copies = []
    for s in range(2):
        copies += message_copies(where, s, right, inverse, lower, main, left)
    started = start_all(copies, sems)
    for s in range(2):
        main[s, B : B + 16, 4 * B : 6 * B] = jnp.zeros((16, 2 * B), jnp.float32)
    for copy in started:
        copy.wait()


def rest_kernel(where, lower, front, dep, couple, fronts, sems):
    rows = rows_of(64 * where[6], 64)
    run_copies(
        [
            (lower.at[:, :, pl.ds(0, 8 * B)], couple),
            (front.at[0], fronts.at[:, pl.ds(0, B)]),
            (front.at[1, :, rows], fronts.at[:, pl.ds(B, 64)]),
        ],
        sems,
    )


def own_kernel(where, main, left, *refs):
    own = refs[-1]
    own[:, :, 0 : 4 * B] = main[:, :, 0 : 4 * B]

    @pl.when(where[0] == 0)
    def _():
        own[:, 0:B, 4 * B :] = left[...]
        own[:, B:, 4 * B :] = jnp.zeros((2, 16, 2 * B), jnp.float32)

    @pl.when(where[0] == 1)
    def _():
        own[:, :, 4 * B :] = main[:, :, 4 * B :]


def pass_kernel(value, dep, out):
    pass


def gate(value, dep):
    return pl.pallas_call(
        pass_kernel,
        out_shape=jax.ShapeDtypeStruct(value.shape, value.dtype),
        in_specs=[AN] * 2,
        out_specs=AN,
        input_output_aliases={0: 0},
        name="gate",
    )(value, dep)


def cut(start, size):
    return pl.ds(pl.multiple_of(start, B), size)


def rows_of(start, size):
    return pl.ds(pl.multiple_of(start, 64), size)


def f32(*shape):
    return jax.ShapeDtypeStruct(shape, jnp.float32)


def pack(where, right, inverse, lower):
    return pl.pallas_call(
        pack_kernel,
        out_shape=[f32(2, B + 16, 6 * B), f32(2, B, 2 * B)],
        in_specs=[SM] + [HB] * 3,
        out_specs=[VM] * 2,
        scratch_shapes=[pltpu.SemaphoreType.DMA((16,))],
        name="pack",
    )(where, right, inverse, lower)


def rest(where, lower, front, dep):
    return pl.pallas_call(
        rest_kernel,
        out_shape=[f32(2, B, 8 * B), f32(8, B + 64, B)],
        in_specs=[SM] + [HB] * 2 + [AN],
        out_specs=[VM] * 2,
        scratch_shapes=[pltpu.SemaphoreType.DMA((3,))],
        name="rest",
    )(where, lower, front, dep)


def own_piece(where, main, left, *dep):
    return pl.pallas_call(
        own_kernel,
        out_shape=f32(2, B + 16, 6 * B),
        in_specs=[SM] + [VM] * 2 + [AN] * len(dep),
        out_specs=VM,
        name="own",
    )(where, main, left, *dep)


def solve_factor(stage, w, matrix):
    def pair_inverse(m):
        i = 2 * m
        k = i % 4
        upper = stage[i, 0:B, 3 * B : 4 * B]
        lower = stage[i + 1, 0:B, 3 * B : 4 * B]
        below = -times(times(lower, stage[i + 1, 0:B, B * k : B * (k + 1)]), upper)
        zeros = jnp.zeros((B, B), jnp.float32)
        return halves(
            jnp.concatenate(
                [jnp.concatenate([upper, zeros], axis=1), jnp.concatenate([below, lower], axis=1)],
                axis=0,
            )
        )

    def block(m, n):
        i = 2 * m
        if m // 2 == n // 2:
            cols = slice(0, 2 * B)
        else:
            i = i - 4 if n == 0 else i
            cols = slice(4 * B, 6 * B)
        return halves(jnp.concatenate([stage[i, 0:B, cols], stage[i + 1, 0:B, cols]], axis=0))

    inverses = [pair_inverse(m) for m in range(4)]
    solved = {}
    for m in (3, 2, 1, 0):
        total = w[:, 2 * B * m : 2 * B * (m + 1)]
        for n in range(m + 1, 4):
            total = total - times(solved[n], block(n, m))
        value = times(total, inverses[m])
        if matrix is not None:
            matrix[:, 2 * B * m : 2 * B * (m + 1)] = value
        solved[m] = halves(value)
    return solved


def coupling_copies(s, w, c, coupling, coupling_other):
    return [
        (coupling.at[s], w.at[cut(B * c, B), :]),
        (coupling_other.at[s], w.at[cut(B * (1 - c), B), :]),
    ]


def front_copies(w, at, front):
    return [(front.at[i], w.at[pl.ds(at, B), pl.ds(B * i, B)]) for i in range(8)]


def shared_copies(w, at, c, mine, theirs):
    copies = []
    for i in range(8):
        cols = pl.ds(B * i, B)
        copies.append((mine.at[i, pl.ds(B, 64)], w.at[rows_of(at + 64 * c, 64), cols]))
        copies.append((theirs.at[i], w.at[rows_of(at + 64 * (1 - c), 64), cols]))
    return copies


def own_rows(w, at, own_row):
    w[at : at + B, :] = jnp.zeros((B, 8 * B), jnp.float32)
    row = lax.broadcasted_iota(jnp.int32, (B, B), 0)
    col = lax.broadcasted_iota(jnp.int32, (B, B), 1)
    w[at : at + B, lanes(own_row)] = jnp.where(row == col, 1.0, 0.0)


def start_all(copies, sems):
    started = [pltpu.make_async_copy(src, dst, sems.at[n]) for n, (src, dst) in enumerate(copies)]
    for copy in started:
        copy.start()
    return started


def factor_kernel(s, where, *refs):
    c = where[6]
    a = where[0]
    y = where[1]
    if s == 0:
        matrix, right, u, stage, w, sems = refs[13:]
        copies = front_copies(w, 2 * B, refs[12])
    else:
        matrix, right, stage, w, sems = refs[15:]
        copies = shared_copies(w, 2 * B, c, *refs[12:14])
    copies += coupling_copies(s, w, c, *refs[10:12])
    own_rows(w, 3 * B, where[4])
    half = (B + 16) // 2
    for g, parts in ((a, refs[0:5]), (1 - a, refs[5:10])):
        parts = [part.at[s] for part in parts]
        copies.append((parts[0], stage.at[4 * g + y]))
        copies.append((parts[1], stage.at[4 * g + lax.rem(y + 3, 4)]))
        copies.append((parts[2], stage.at[4 * g + lax.rem(y + 1, 4)]))
        far = 4 * g + lax.rem(y + 2, 4)
        copies.append((parts[3], stage.at[far, pl.ds(0, half)]))
        copies.append((parts[4], stage.at[far, pl.ds(half, half)]))
    for copy in start_all(copies, sems):
        copy.wait()
    solved = solve_factor(stage, w, matrix)
    for i in range(8):
        for k in range(4):
            right[16 * k : 16 * k + 16, B * i : B * (i + 1)] = stage[i, B : B + 16, B * k : B * (k + 1)]
    if s == 1:
        return
    total = None
    for m in range(4):
        high, low = solved[m]
        part = (high[0 : 2 * B], low[0 : 2 * B])
        part = times(right[:, 2 * B * m : 2 * B * (m + 1)], part, NT)
        total = part if total is None else total + part
    u[...] = total


def factor(s, where, pieces):
    shapes = [f32(4 * B, 8 * B), f32(64, 8 * B)]
    if s == 0:
        shapes.append(f32(64, 2 * B))
    return pl.pallas_call(
        partial(factor_kernel, s),
        out_shape=shapes,
        in_specs=[SM] + [HB] * len(pieces),
        out_specs=[VM] * len(shapes),
        scratch_shapes=[
            pltpu.VMEM((8, B + 16, 6 * B), jnp.float32),
            pltpu.VMEM((4 * B, 8 * B), jnp.float32),
            pltpu.SemaphoreType.DMA((28,)),
        ],
        compiler_params=pltpu.CompilerParams(vmem_limit_bytes=32 * 2**20),
        name="factor",
    )(where, *pieces)


def apply_matrix(target, matrix, rows):
    total = None
    for m in range(4):
        cols = slice(2 * B * m, 2 * B * (m + 1))
        part = times(target[:, cols], matrix[rows, cols], NT)
        total = part if total is None else total + part
    return total


def bottom_kernel(where, target, matrix, u0, u1, u2, u3, *refs):
    front, solved, t = refs[-3:]
    y = where[1]
    for k, u in enumerate((u0, u1, u2, u3)):
        col = lax.rem(y + 4 - k, 4)
        for g in range(2):
            at = lanes(4 * g + col)
            t[:, at] = target[:, at] - u[:, B * g : B * (g + 1)]
    last = matrix.shape[0]
    value = apply_matrix(t, matrix, slice(last - 2 * B, last))
    for k in range(16):
        front[k] = value[:, 0:B]
    solved[...] = value[:, B : 2 * B]


def bottom(where, target, matrix, received, *dep):
    return pl.pallas_call(
        bottom_kernel,
        out_shape=[
            jax.ShapeDtypeStruct((16, 64, B), jnp.float32),
            jax.ShapeDtypeStruct((64, B), jnp.float32),
        ],
        in_specs=[SM] + [VM] * 6 + [AN] * len(dep),
        out_specs=[VM] * 2,
        scratch_shapes=[pltpu.VMEM((64, 8 * B), jnp.float32)],
        compiler_params=pltpu.CompilerParams(vmem_limit_bytes=20 * 2**20),
        name="bottom",
    )(where, target, matrix, *received, *dep)


def thirds(value):
    high, rest = halves(value)
    middle = value - high.astype(jnp.float32)
    low = (middle - rest.astype(jnp.float32)).astype(jnp.bfloat16)
    return jnp.concatenate([high, rest, low], axis=0)


def spread(values, index, base, width):
    lhs = jnp.concatenate([thirds(v) for v in values], axis=1)
    col = lax.broadcasted_iota(jnp.int32, (index.shape[0], width), 1) + base
    chosen = jnp.where(index == col, 1.0, 0.0).astype(jnp.bfloat16)
    laid = dot(lhs, chosen)
    n = values[0].shape[0]
    return laid[0:n] + (laid[n : 2 * n] + laid[2 * n : 3 * n])


def first_fronts(c, mine, theirs):
    for q in range(2):
        for e, (upper, lower) in enumerate(((mine, theirs), (theirs, mine))):
            group = c if e == 0 else 1 - c
            for y in (0, 2):
                values = [upper[4 * q + k] + lower[4 * (3 - q) + k] for k in (y, y + 1)]
                yield values, cut(1024 * q + 512 * group + B * y, 2 * B)


def middle_kernel(where, target, matrix, mine, theirs, index, t_out, u):
    base = 2 * 2048 + where[2] * 1024
    total = target[...]
    for values, rows in first_fronts(where[6], mine, theirs):
        total = total - spread(values, index[rows, :], base, 8 * B)
    t_out[...] = total
    u[...] = apply_matrix(total, matrix, slice(0, 2 * B))


def middle(where, target, matrix, mine, theirs, index):
    return pl.pallas_call(
        middle_kernel,
        out_shape=[
            jax.ShapeDtypeStruct((64, 8 * B), jnp.float32),
            jax.ShapeDtypeStruct((64, 2 * B), jnp.float32),
        ],
        in_specs=[SM] + [VM] * 5,
        out_specs=[VM] * 2,
        compiler_params=pltpu.CompilerParams(vmem_limit_bytes=24 * 2**20),
        name="middle",
    )(where, target, matrix, mine, theirs, index)


def older_kernel(where, mine, theirs, index, out):
    for t in range(2):
        total = None
        for values, rows in first_fronts(where[6], mine, theirs):
            part = spread(values, index[rows, :], t * 2048 + where[3] * B, B)
            total = part if total is None else total + part
        out[t] = total


def older(where, mine, theirs, index):
    return pl.pallas_call(
        older_kernel,
        out_shape=f32(2, 64, B),
        in_specs=[SM] + [VM] * 3,
        out_specs=VM,
        compiler_params=pltpu.CompilerParams(vmem_limit_bytes=24 * 2**20),
        name="older",
    )(where, mine, theirs, index)


def last_kernel(where, held, mine, index, out):
    for t in range(2):
        total = held[t]
        for j in range(0, 8, 2):
            values = [mine[k] + mine[8 + k] for k in (j, j + 1)]
            total = total + spread(values, index[B * j : B * (j + 2), :], t * 2048 + where[3] * B, B)
        out[t] = total


def last(where, held, mine, index):
    return pl.pallas_call(
        last_kernel,
        out_shape=f32(2, 64, B),
        in_specs=[SM] + [VM] * 3,
        out_specs=VM,
        compiler_params=pltpu.CompilerParams(vmem_limit_bytes=24 * 2**20),
        name="last",
    )(where, held, mine, index)


HALVES = [list(range(8)), list(range(8, 16))]


def on_device(right_side, diag_inverse, sep_lower, front_lower, front_index):
    leaf = lax.axis_index("leaf")
    here = lax.axis_index("rows")
    c = lax.rem(leaf, 2)
    z = here // 4
    y = lax.rem(here, 4)
    h = z // 2
    odd = lax.rem(z, 2)
    a = lax.rem(c + h, 2)
    where = jnp.stack([a, y, h, here, 4 * a + y, odd, c, 4 * odd + y]).astype(jnp.int32)

    right, inverse, lower, front = right_side[0], diag_inverse[0], sep_lower[0], front_lower[0]
    front = front.reshape(2, 8, B, B)

    index = front_index[0, 0]
    index_other = send(index, to_core)
    index0 = jnp.where(
        c == 0,
        jnp.concatenate([index, index_other]),
        jnp.concatenate([index_other, index]),
    )[:, None]
    index1 = front_index[0, 1][:, None]

    main, left = pack(where, right, inverse, lower)
    couple, fronts = rest(where, lower, front, main)
    main = send(main, to_line)
    left = send(left, left_to_line)
    own = own_piece(where, main, left, couple, fronts, index0, index1)
    size = own.shape[1] // 2
    up = send(own, along(1))
    down = send(own, along(3))
    far_low = send(up[:, :size], along(1))
    far_high = send(down[:, size:], along(3))
    pieces = [own, up, down, far_low, far_high]
    pieces += [send(p, to_core) for p in pieces]
    couple = send(couple, coupling_to_top)
    pieces += [couple, send(couple, to_core)]
    fronts = lax.all_to_all(fronts, "rows", 0, 0, axis_index_groups=HALVES, tiled=True)
    front0 = send(fronts[:, :B], to_line)
    front1 = send(fronts[:, B:], to_core)

    matrix0, target0, u0 = factor(0, where, [*pieces, front0])
    received = [send(u0, top_to_bottom(k)) for k in range(4)]
    matrix1, target1 = factor(1, where, [*pieces, fronts, front1, u0])
    done0, solved0 = bottom(where, target0, matrix0, received, target1)
    mine0 = lax.all_to_all(done0, "rows", 0, 0, tiled=True)
    theirs0 = send(mine0, to_core)

    target1, u1 = middle(where, target1, matrix1, mine0, theirs0, index0)
    received = [send(u1, top_to_bottom(k)) for k in range(4)]
    done1, solved1 = bottom(where, target1, matrix1, received)
    mine1 = lax.all_to_all(done1, "rows", 0, 0, tiled=True)
    top = last(where, older(where, mine0, theirs0, index0), mine1, index1)
    solved = send(jnp.stack([solved0, solved1]), to_line)
    return solved[None], top[None]


def solution(mesh):
    in_specs = (
        P("leaf", None, None, "rows"),
        P("leaf", None, "rows", None),
        P("leaf", None, "rows", None),
        P("leaf", None, None, "rows"),
        P("leaf", None, None),
    )
    out_specs = (P("leaf", None, None, "rows"), P("leaf", None, None, "rows"))
    return jax.shard_map(
        on_device, mesh=mesh, in_specs=in_specs, out_specs=out_specs, check_vma=False
    )
```

```python
from functools import partial

import jax
import jax.numpy as jnp
from jax import lax
from jax.experimental import pallas as pl
from jax.experimental.pallas import tpu as pltpu
from jax.sharding import PartitionSpec as P

AXES = ("leaf", "rows")
VM = pl.BlockSpec(memory_space=pltpu.VMEM)
HB = pl.BlockSpec(memory_space=pltpu.HBM)
AN = pl.BlockSpec(memory_space=pl.ANY)
SM = pl.BlockSpec(memory_space=pltpu.SMEM)
B = 128
NT = (((1,), (1,)), ((), ()))
NN = (((1,), (0,)), ((), ()))


def place(x, c, z, y):
    return (2 * x + c) * 16 + 4 * z + y % 4


def pairs(rule):
    found = []
    for x in range(4):
        for c in range(2):
            for z in range(4):
                for y in range(4):
                    there = rule(c, z, y)
                    if there is not None:
                        found.append((place(x, c, z, y), place(x, *there)))
    return found


def send(value, rule):
    return lax.ppermute(value, AXES, pairs(rule))


def to_line(c, z, y):
    h = z // 2
    return ((z % 2) ^ h, 2 * h + (c ^ h), y)


def left_to_line(c, z, y):
    h = z // 2
    return (h, 2 * h + (c ^ h), y) if z % 2 == 1 else None


def to_core(c, z, y):
    return (1 - c, z, y)


def along(k):
    def rule(c, z, y):
        return (c, z, y + k)

    return rule


def coupling_to_top(c, z, y):
    return (z - 2, c, y) if z >= 2 else None


def top_to_bottom(k):
    def rule(c, z, y):
        return (c, 3 - z, y + k) if z < 2 else None

    return rule


def halves(value):
    high = value.astype(jnp.bfloat16)
    low = (value - high.astype(jnp.float32)).astype(jnp.bfloat16)
    return high, low


def dot(left, right, dims=NN):
    return lax.dot_general(left, right, dims, preferred_element_type=jnp.float32)


def times(left, right, dims=NN):
    lh, ll = left if isinstance(left, tuple) else halves(left)
    rh, rl = right if isinstance(right, tuple) else halves(right)
    return dot(lh, rh, dims) + (dot(lh, rl, dims) + dot(ll, rh, dims))


def lanes(block):
    return pl.ds(pl.multiple_of(block * B, B), B)


def run_copies(copies, sems):
    for copy in start_all(copies, sems):
        copy.wait()


def message_copies(where, s, right, inverse, lower, main, left):
    base = 1024 * where[2]
    cols = pl.ds(0, B)
    copies = [
        (lower.at[s, :, cut(base + 512 * where[5], 3 * B)], main.at[s, cols, pl.ds(0, 3 * B)]),
        (inverse.at[s], main.at[s, cols, pl.ds(3 * B, B)]),
        (lower.at[s, :, cut(base + 256, 2 * B)], main.at[s, cols, pl.ds(4 * B, 2 * B)]),
        (lower.at[s, :, cut(base, 2 * B)], left.at[s]),
    ]
    for k in range(4):
        copies.append((right.at[s, pl.ds(16 * k, 16)], main.at[s, pl.ds(B, 16), pl.ds(B * k, B)]))
    return copies


def pack_kernel(where, right, inverse, lower, main, left, sems):
    copies = []
    for s in range(2):
        copies += message_copies(where, s, right, inverse, lower, main, left)
    started = start_all(copies, sems)
    for s in range(2):
        main[s, B : B + 16, 4 * B : 6 * B] = jnp.zeros((16, 2 * B), jnp.float32)
    for copy in started:
        copy.wait()


def rest_kernel(where, lower, front, dep, couple, fronts, sems):
    rows = rows_of(64 * where[6], 64)
    run_copies(
        [
            (lower.at[:, :, pl.ds(0, 8 * B)], couple),
            (front.at[0], fronts.at[:, pl.ds(0, B)]),
            (front.at[1, :, rows], fronts.at[:, pl.ds(B, 64)]),
        ],
        sems,
    )


def own_kernel(where, main, left, *refs):
    own = refs[-1]
    own[:, :, 0 : 4 * B] = main[:, :, 0 : 4 * B]

    @pl.when(where[0] == 0)
    def _():
        own[:, 0:B, 4 * B :] = left[...]
        own[:, B:, 4 * B :] = jnp.zeros((2, 16, 2 * B), jnp.float32)

    @pl.when(where[0] == 1)
    def _():
        own[:, :, 4 * B :] = main[:, :, 4 * B :]


def pass_kernel(value, dep, out):
    pass


def gate(value, dep):
    return pl.pallas_call(
        pass_kernel,
        out_shape=jax.ShapeDtypeStruct(value.shape, value.dtype),
        in_specs=[AN] * 2,
        out_specs=AN,
        input_output_aliases={0: 0},
        name="gate",
    )(value, dep)


def cut(start, size):
    return pl.ds(pl.multiple_of(start, B), size)


def rows_of(start, size):
    return pl.ds(pl.multiple_of(start, 64), size)


def f32(*shape):
    return jax.ShapeDtypeStruct(shape, jnp.float32)


def pack(where, right, inverse, lower):
    return pl.pallas_call(
        pack_kernel,
        out_shape=[f32(2, B + 16, 6 * B), f32(2, B, 2 * B)],
        in_specs=[SM] + [HB] * 3,
        out_specs=[VM] * 2,
        scratch_shapes=[pltpu.SemaphoreType.DMA((16,))],
        name="pack",
    )(where, right, inverse, lower)


def rest(where, lower, front, dep):
    return pl.pallas_call(
        rest_kernel,
        out_shape=[f32(2, B, 8 * B), f32(8, B + 64, B)],
        in_specs=[SM] + [HB] * 2 + [AN],
        out_specs=[VM] * 2,
        scratch_shapes=[pltpu.SemaphoreType.DMA((3,))],
        name="rest",
    )(where, lower, front, dep)


def own_piece(where, main, left, *dep):
    return pl.pallas_call(
        own_kernel,
        out_shape=f32(2, B + 16, 6 * B),
        in_specs=[SM] + [VM] * 2 + [AN] * len(dep),
        out_specs=VM,
        name="own",
    )(where, main, left, *dep)


def solve_factor(stage, w, matrix, rows_here):
    def pair_inverse(m):
        i = 2 * m
        k = i % 4
        upper = stage[i, 0:B, 3 * B : 4 * B]
        lower = stage[i + 1, 0:B, 3 * B : 4 * B]
        below = -times(times(lower, stage[i + 1, 0:B, B * k : B * (k + 1)]), upper)
        zeros = jnp.zeros((B, B), jnp.float32)
        return halves(
            jnp.concatenate(
                [jnp.concatenate([upper, zeros], axis=1), jnp.concatenate([below, lower], axis=1)],
                axis=0,
            )
        )

    def block(m, n):
        i = 2 * m
        if m // 2 == n // 2:
            cols = slice(0, 2 * B)
        else:
            i = i - 4 if n == 0 else i
            cols = slice(4 * B, 6 * B)
        return halves(jnp.concatenate([stage[i, 0:B, cols], stage[i + 1, 0:B, cols]], axis=0))

    inverses = [pair_inverse(m) for m in range(4)]
    for copy in rows_here:
        copy.wait()
    solved = {}
    for m in (3, 2, 1, 0):
        total = w[:, 2 * B * m : 2 * B * (m + 1)]
        for n in range(m + 1, 4):
            total = total - times(solved[n], block(n, m))
        value = times(total, inverses[m])
        if matrix is not None:
            matrix[:, 2 * B * m : 2 * B * (m + 1)] = value
        solved[m] = halves(value)
    return solved


def coupling_copies(s, w, c, coupling, coupling_other):
    return [
        (coupling.at[s], w.at[cut(B * c, B), :]),
        (coupling_other.at[s], w.at[cut(B * (1 - c), B), :]),
    ]


def front_copies(w, at, front):
    return [(front.at[i], w.at[pl.ds(at, B), pl.ds(B * i, B)]) for i in range(8)]


def shared_copies(w, at, c, mine, theirs):
    copies = []
    for i in range(8):
        cols = pl.ds(B * i, B)
        copies.append((mine.at[i, pl.ds(B, 64)], w.at[rows_of(at + 64 * c, 64), cols]))
        copies.append((theirs.at[i], w.at[rows_of(at + 64 * (1 - c), 64), cols]))
    return copies


def own_rows(w, at, own_row):
    w[at : at + B, :] = jnp.zeros((B, 8 * B), jnp.float32)
    row = lax.broadcasted_iota(jnp.int32, (B, B), 0)
    col = lax.broadcasted_iota(jnp.int32, (B, B), 1)
    w[at : at + B, lanes(own_row)] = jnp.where(row == col, 1.0, 0.0)


def start_all(copies, sems):
    started = [pltpu.make_async_copy(src, dst, sems.at[n]) for n, (src, dst) in enumerate(copies)]
    for copy in started:
        copy.start()
    return started


def factor_kernel(s, where, *refs):
    c = where[6]
    a = where[0]
    y = where[1]
    if s == 0:
        matrix, right, u, stage, w, sems = refs[13:]
        copies = front_copies(w, 2 * B, refs[12])
    else:
        matrix, right, stage, w, sems = refs[15:]
        copies = shared_copies(w, 2 * B, c, *refs[12:14])
    copies += coupling_copies(s, w, c, *refs[10:12])
    own_rows(w, 3 * B, where[4])
    rows = len(copies)
    half = (B + 16) // 2
    for g, parts in ((a, refs[0:5]), (1 - a, refs[5:10])):
        parts = [part.at[s] for part in parts]
        copies.append((parts[0], stage.at[4 * g + y]))
        copies.append((parts[1], stage.at[4 * g + lax.rem(y + 3, 4)]))
        copies.append((parts[2], stage.at[4 * g + lax.rem(y + 1, 4)]))
        far = 4 * g + lax.rem(y + 2, 4)
        copies.append((parts[3], stage.at[far, pl.ds(0, half)]))
        copies.append((parts[4], stage.at[far, pl.ds(half, half)]))
    started = start_all(copies, sems)
    for copy in started[rows:]:
        copy.wait()
    solved = solve_factor(stage, w, matrix, started[:rows])
    for i in range(8):
        for k in range(4):
            right[16 * k : 16 * k + 16, B * i : B * (i + 1)] = stage[i, B : B + 16, B * k : B * (k + 1)]
    if s == 1:
        return
    total = None
    for m in range(4):
        high, low = solved[m]
        part = (high[0 : 2 * B], low[0 : 2 * B])
        part = times(right[:, 2 * B * m : 2 * B * (m + 1)], part, NT)
        total = part if total is None else total + part
    u[...] = total


def factor(s, where, pieces):
    shapes = [f32(4 * B, 8 * B), f32(64, 8 * B)]
    if s == 0:
        shapes.append(f32(64, 2 * B))
    return pl.pallas_call(
        partial(factor_kernel, s),
        out_shape=shapes,
        in_specs=[SM] + [HB] * len(pieces),
        out_specs=[VM] * len(shapes),
        scratch_shapes=[
            pltpu.VMEM((8, B + 16, 6 * B), jnp.float32),
            pltpu.VMEM((4 * B, 8 * B), jnp.float32),
            pltpu.SemaphoreType.DMA((28,)),
        ],
        compiler_params=pltpu.CompilerParams(vmem_limit_bytes=32 * 2**20),
        name="factor",
    )(where, *pieces)


def apply_matrix(target, matrix, rows):
    total = None
    for m in range(4):
        cols = slice(2 * B * m, 2 * B * (m + 1))
        part = times(target[:, cols], matrix[rows, cols], NT)
        total = part if total is None else total + part
    return total


def bottom_kernel(where, target, matrix, u0, u1, u2, u3, *refs):
    front, solved, t = refs[-3:]
    y = where[1]
    for k, u in enumerate((u0, u1, u2, u3)):
        col = lax.rem(y + 4 - k, 4)
        for g in range(2):
            at = lanes(4 * g + col)
            t[:, at] = target[:, at] - u[:, B * g : B * (g + 1)]
    last = matrix.shape[0]
    value = apply_matrix(t, matrix, slice(last - 2 * B, last))
    for k in range(16):
        front[k] = value[:, 0:B]
    solved[...] = value[:, B : 2 * B]


def bottom(where, target, matrix, received, *dep):
    return pl.pallas_call(
        bottom_kernel,
        out_shape=[
            jax.ShapeDtypeStruct((16, 64, B), jnp.float32),
            jax.ShapeDtypeStruct((64, B), jnp.float32),
        ],
        in_specs=[SM] + [VM] * 6 + [AN] * len(dep),
        out_specs=[VM] * 2,
        scratch_shapes=[pltpu.VMEM((64, 8 * B), jnp.float32)],
        compiler_params=pltpu.CompilerParams(vmem_limit_bytes=20 * 2**20),
        name="bottom",
    )(where, target, matrix, *received, *dep)


def thirds(value):
    high, rest = halves(value)
    middle = value - high.astype(jnp.float32)
    low = (middle - rest.astype(jnp.float32)).astype(jnp.bfloat16)
    return jnp.concatenate([high, rest, low], axis=0)


def spread(values, index, base, width):
    lhs = jnp.concatenate([thirds(v) for v in values], axis=1)
    col = lax.broadcasted_iota(jnp.int32, (index.shape[0], width), 1) + base
    chosen = jnp.where(index == col, 1.0, 0.0).astype(jnp.bfloat16)
    laid = dot(lhs, chosen)
    n = values[0].shape[0]
    return laid[0:n] + (laid[n : 2 * n] + laid[2 * n : 3 * n])


def first_fronts(c, mine, theirs):
    for q in range(2):
        for e, (upper, lower) in enumerate(((mine, theirs), (theirs, mine))):
            group = c if e == 0 else 1 - c
            for y in (0, 2):
                values = [upper[4 * q + k] + lower[4 * (3 - q) + k] for k in (y, y + 1)]
                yield values, cut(1024 * q + 512 * group + B * y, 2 * B)


def middle_kernel(where, target, matrix, mine, theirs, index, t_out, u):
    base = 2 * 2048 + where[2] * 1024
    total = target[...]
    for values, rows in first_fronts(where[6], mine, theirs):
        total = total - spread(values, index[rows, :], base, 8 * B)
    t_out[...] = total
    u[...] = apply_matrix(total, matrix, slice(0, 2 * B))


def middle(where, target, matrix, mine, theirs, index):
    return pl.pallas_call(
        middle_kernel,
        out_shape=[
            jax.ShapeDtypeStruct((64, 8 * B), jnp.float32),
            jax.ShapeDtypeStruct((64, 2 * B), jnp.float32),
        ],
        in_specs=[SM] + [VM] * 5,
        out_specs=[VM] * 2,
        compiler_params=pltpu.CompilerParams(vmem_limit_bytes=24 * 2**20),
        name="middle",
    )(where, target, matrix, mine, theirs, index)


def older_kernel(where, mine, theirs, index, out):
    for t in range(2):
        total = None
        for values, rows in first_fronts(where[6], mine, theirs):
            part = spread(values, index[rows, :], t * 2048 + where[3] * B, B)
            total = part if total is None else total + part
        out[t] = total


def older(where, mine, theirs, index):
    return pl.pallas_call(
        older_kernel,
        out_shape=f32(2, 64, B),
        in_specs=[SM] + [VM] * 3,
        out_specs=VM,
        compiler_params=pltpu.CompilerParams(vmem_limit_bytes=24 * 2**20),
        name="older",
    )(where, mine, theirs, index)


def last_kernel(where, held, mine, index, out):
    for t in range(2):
        total = held[t]
        for j in range(0, 8, 2):
            values = [mine[k] + mine[8 + k] for k in (j, j + 1)]
            total = total + spread(values, index[B * j : B * (j + 2), :], t * 2048 + where[3] * B, B)
        out[t] = total


def last(where, held, mine, index):
    return pl.pallas_call(
        last_kernel,
        out_shape=f32(2, 64, B),
        in_specs=[SM] + [VM] * 3,
        out_specs=VM,
        compiler_params=pltpu.CompilerParams(vmem_limit_bytes=24 * 2**20),
        name="last",
    )(where, held, mine, index)


HALVES = [list(range(8)), list(range(8, 16))]


def on_device(right_side, diag_inverse, sep_lower, front_lower, front_index):
    leaf = lax.axis_index("leaf")
    here = lax.axis_index("rows")
    c = lax.rem(leaf, 2)
    z = here // 4
    y = lax.rem(here, 4)
    h = z // 2
    odd = lax.rem(z, 2)
    a = lax.rem(c + h, 2)
    where = jnp.stack([a, y, h, here, 4 * a + y, odd, c, 4 * odd + y]).astype(jnp.int32)

    right, inverse, lower, front = right_side[0], diag_inverse[0], sep_lower[0], front_lower[0]
    front = front.reshape(2, 8, B, B)

    index = front_index[0, 0]
    index_other = send(index, to_core)
    index0 = jnp.where(
        c == 0,
        jnp.concatenate([index, index_other]),
        jnp.concatenate([index_other, index]),
    )[:, None]
    index1 = front_index[0, 1][:, None]

    main, left = pack(where, right, inverse, lower)
    couple, fronts = rest(where, lower, front, main)
    main = send(main, to_line)
    left = send(left, left_to_line)
    own = own_piece(where, main, left, couple, fronts, index0, index1)
    size = own.shape[1] // 2
    up = send(own, along(1))
    down = send(own, along(3))
    far_low = send(up[:, :size], along(1))
    far_high = send(down[:, size:], along(3))
    pieces = [own, up, down, far_low, far_high]
    pieces += [send(p, to_core) for p in pieces]
    couple = send(couple, coupling_to_top)
    pieces += [couple, send(couple, to_core)]
    fronts = lax.all_to_all(fronts, "rows", 0, 0, axis_index_groups=HALVES, tiled=True)
    front0 = send(fronts[:, :B], to_line)
    front1 = send(fronts[:, B:], to_core)

    matrix0, target0, u0 = factor(0, where, [*pieces, front0])
    received = [send(u0, top_to_bottom(k)) for k in range(4)]
    matrix1, target1 = factor(1, where, [*pieces, fronts, front1, u0])
    done0, solved0 = bottom(where, target0, matrix0, received, target1)
    mine0 = lax.all_to_all(done0, "rows", 0, 0, tiled=True)
    theirs0 = send(mine0, to_core)

    target1, u1 = middle(where, target1, matrix1, mine0, theirs0, index0)
    received = [send(u1, top_to_bottom(k)) for k in range(4)]
    done1, solved1 = bottom(where, target1, matrix1, received)
    mine1 = lax.all_to_all(done1, "rows", 0, 0, tiled=True)
    top = last(where, older(where, mine0, theirs0, index0), mine1, index1)
    solved = send(jnp.stack([solved0, solved1]), to_line)
    return solved[None], top[None]


def solution(mesh):
    in_specs = (
        P("leaf", None, None, "rows"),
        P("leaf", None, "rows", None),
        P("leaf", None, "rows", None),
        P("leaf", None, None, "rows"),
        P("leaf", None, None),
    )
    out_specs = (P("leaf", None, None, "rows"), P("leaf", None, None, "rows"))
    return jax.shard_map(
        on_device, mesh=mesh, in_specs=in_specs, out_specs=out_specs, check_vma=False
    )
```
